256 devices in a mesh: chan: 8 (over x, core), beam: 32 (over y, z).
Axes of the slice: x: 4, y: 4, z: 8, core: 2. Of those that a mesh axis runs over, the one named last changes fastest.
Arguments:
- voltages: bfloat16 [1024, 4, 2, 2, 256, 128], P('chan', None, None, None, 'beam'), may hold values from -6 to 6
- bin_range: int32 [2, 256, 1024], P(None, 'beam', 'chan'), may hold values from 0 to 508, as said below
- weights: float32 [4, 256, 1024], P(None, 'beam', 'chan'), may hold values from 0.2 to 1
- bandpass: float32 [1024], P('chan'), may hold values from 0.4 to 18, as said below
Outputs:
- sky_beams: float32 [8, 4, 256, 1024], P(None, None, 'beam', 'chan')
The draws below stay inside these ranges and needn't reach their ends.
Inputs may be any that keep to these rules, and one draw needn't show every extreme that they name: bin_range[0, j, c] is the first north-south bin of sky beam j in channel c and bin_range[1, j, c] its number of bins, 1 to 4; the first bin plus 4 stays within 512. `bandpass`: positive.
All inputs are finite; a program needn't handle non-finite values.
Results may differ from the reference program's by a relative error of at most 0.0009.
Values may be sent and summed in bfloat16 or wider, within the bound.
No kernel may reach another device: no remote copies, remote signals or barrier semaphores. Data moves between devices by JAX's collectives and lax.ppermute only.
A program may use at most 64 MiB of HBM per device.

```python
import math
import jax
import jax.numpy as jnp
from jax import lax

CHANNELS = 1024
FEEDS = 256
CYL = 4
NSBIN = 512
NSBEAM = 256
POL = 2
SAMPLES = 128
FLEN = 16
MAXBIN = 4


def draw_bin_range(key, part):
    key = jax.random.fold_in(key, 11)
    key_start, key_count = jax.random.split(key)
    beam_idx = jnp.arange(NSBEAM, dtype=jnp.int32)[:, None]
    chan_idx = jnp.arange(CHANNELS, dtype=jnp.int32)[None, :]
    centre_bin = beam_idx * NSBIN * (2 * CHANNELS - chan_idx) // (NSBEAM * 2 * CHANNELS)
    jitter = jax.random.randint(key_start, (NSBEAM, CHANNELS), 0, 2, dtype=jnp.int32)
    first_bin = jnp.clip(centre_bin + jitter, 0, NSBIN - MAXBIN)
    reach = 1 + (MAXBIN - 1) * (CHANNELS - chan_idx) // CHANNELS
    raw_count = jax.random.randint(key_count, (NSBEAM, CHANNELS), 0, MAXBIN, dtype=jnp.int32)
    bin_count = 1 + raw_count % reach
    bin_count = jnp.where(beam_idx % 8 == 0, MAXBIN, bin_count)
    return jnp.stack([first_bin, bin_count], axis=0).astype(jnp.int32)


def draw_bandpass(key, part):
    key = jax.random.fold_in(key, 23)
    rising = 1.0 + 2.0 * jnp.arange(CHANNELS, dtype=jnp.float32) / (CHANNELS - 1)
    factor = jnp.exp(jax.random.uniform(key, (CHANNELS,), jnp.float32, -0.7, 0.7))
    return (rising * factor).astype(jnp.float32)


def shard_levels(rng, dims, pieces, smallest, high):
    loudness, own = 1.0, jax.random.fold_in(rng, 6)
    for dim, blocks in pieces:
        steps = jnp.exp(jax.random.uniform(jax.random.fold_in(own, dim), (blocks,), jnp.float32, smallest / len(pieces), high / len(pieces)))
        loudness = loudness * jnp.repeat(steps, dims[dim] // blocks).reshape([-1 if axis == dim else 1 for axis in range(len(dims))])
    return loudness


def gaussian(own_key, extent, deviation, limit, shards=(), kind=jnp.bfloat16):
    values = deviation * jax.random.normal(own_key, extent, jnp.float32)
    if shards:
        values = values * shard_levels(own_key, extent, shards, -0.22, 0.18)
    return jnp.clip(values, -limit, limit).astype(kind)


def setup_inputs(seed: int = 0) -> dict:
    streams_of = jax.random.split(jax.random.key(seed), 5)
    return {
        "voltages": gaussian(streams_of[0], (CHANNELS, CYL, POL, 2, FEEDS, SAMPLES), 1.0, 6.0, ((0, 8), (4, 32))),
        "bin_range": draw_bin_range(jax.random.fold_in(streams_of[4], 71), 0),
        "weights": jnp.clip(0.2 + 0.8 * jax.random.uniform(streams_of[2], (MAXBIN, NSBEAM, CHANNELS), jnp.float32) ** shard_levels(streams_of[2], (MAXBIN, NSBEAM, CHANNELS), ((1, 32), (2, 8)), -0.2, 0.2), 0.2, 1.0),
        "bandpass": draw_bandpass(jax.random.fold_in(streams_of[4], 71), 0),
    }


def ew_transform(channel_data):
    cylinder = jnp.arange(4, dtype=jnp.int32)
    phases = cylinder[:, None] * cylinder[None, :] % 4
    cosine = jnp.where(phases == 0, 0.5, jnp.where(phases == 2, -0.5, 0.0)).astype(jnp.float32)
    sine_part = jnp.where(phases == 1, 0.5, jnp.where(phases == 3, -0.5, 0.0)).astype(jnp.float32)
    values = channel_data.astype(jnp.float32)
    real_in = values[:, :, 0]
    imag_in = values[:, :, 1]
    highest = lax.Precision.HIGHEST
    real_out = jnp.einsum('ke,epft->kpft', cosine, real_in, precision=highest) + jnp.einsum('ke,epft->kpft', sine_part, imag_in, precision=highest)
    imag_out = jnp.einsum('ke,epft->kpft', cosine, imag_in, precision=highest) - jnp.einsum('ke,epft->kpft', sine_part, real_in, precision=highest)
    return jnp.stack([real_out, imag_out], axis=2)

def ns_table(feed_count, bin_total):
    feed_idx = jnp.arange(feed_count, dtype=jnp.int32)
    bin_idx = jnp.arange(bin_total, dtype=jnp.int32)
    phases = feed_idx[:, None] * bin_idx[None, :] % bin_total
    angles = phases.astype(jnp.float32) * (2.0 * math.pi / bin_total)
    norm_scale = 1.0 / math.sqrt(feed_count)
    cosine = jnp.cos(angles) * norm_scale
    sine_part = jnp.sin(angles) * norm_scale
    first_row = jnp.stack([cosine, -sine_part], axis=1)
    second_row = jnp.stack([sine_part, cosine], axis=1)
    return jnp.stack([first_row, second_row], axis=0).astype(jnp.bfloat16)

def frame_power(spectra):
    squared = lax.optimization_barrier(jnp.sum(spectra * spectra, axis=3))
    ew_count, pol_count, sample_count, bin_total = squared.shape
    framed = squared.reshape(ew_count, pol_count, sample_count // FLEN, FLEN, bin_total)
    return lax.optimization_barrier(jnp.sum(framed, axis=3))

def regrid(power_bins, ranges, tile_weights):
    bin_total = power_bins.shape[-1]
    max_bins = tile_weights.shape[0]
    offsets = jnp.arange(max_bins, dtype=jnp.int32)[:, None, None]
    bin_pos = ranges[0][None] + offsets
    in_range = offsets < ranges[1][None]
    live_weights = jnp.where(in_range, tile_weights, 0.0)
    matches = jnp.arange(bin_total, dtype=jnp.int32)[None, :, None, None] == bin_pos[:, None]
    bin_grid = lax.optimization_barrier(jnp.sum(jnp.where(matches, live_weights[:, None], 0.0), axis=0))
    return jnp.einsum('ckqb,bjc->qkjc', power_bins, bin_grid, precision=lax.Precision.HIGHEST)

def reference(voltages, bin_range, weights, bandpass):
    bin_table = ns_table(FEEDS, NSBIN)

    def per_channel(channel_data):
        ew_beams = ew_transform(channel_data).astype(jnp.bfloat16)
        ew_beams = lax.optimization_barrier(ew_beams)
        spectra = jnp.einsum('kprft,rfsb->kptsb', ew_beams.astype(jnp.float32), bin_table.astype(jnp.float32), precision=lax.Precision.HIGHEST)
        return lax.optimization_barrier(jnp.sum(frame_power(spectra), axis=1))
    power_bins = lax.map(per_channel, voltages) / (2.0 * FLEN)

    def per_tile(inputs):
        power_one, range_one, weight_one = inputs
        return regrid(power_one[None], range_one[..., None], weight_one[..., None])[..., 0]
    beams = lax.map(per_tile, (power_bins, jnp.moveaxis(bin_range, -1, 0), jnp.moveaxis(weights, -1, 0)))
    beams = jnp.transpose(beams, (1, 2, 3, 0)) * bandpass
    band_level = lax.optimization_barrier(jnp.sum(beams, axis=3)) / CHANNELS + 1e-06
    return beams / band_level[..., None]
```

```python
import math

import jax
import jax.numpy as jnp
from jax import lax
from jax.experimental import pallas as pl
from jax.experimental.pallas import tpu as pltpu
from jax.sharding import PartitionSpec as P

CHANNELS = 1024
FEEDS = 256
NSBIN = 512
NSBEAM = 256
FLEN = 16
MAXBIN = 4
TILE = 8
YDIM, ZDIM = 4, 8
PEERS = YDIM * ZDIM
OWNED = 4
ROWS = 128
VMEM_LIMIT = 24 * 1024 * 1024


def split_bf16(values):
    high = values.astype(jnp.bfloat16)
    low = (values - high.astype(jnp.float32)).astype(jnp.bfloat16)
    return high, low


def ns_table():
    row = jnp.arange(NSBIN, dtype=jnp.int32)[:, None]
    feed = jnp.arange(FEEDS, dtype=jnp.int32)[None]
    half = NSBIN // 2
    bins = jnp.where(row <= half, row, row - half)
    angles = (feed * bins % NSBIN).astype(jnp.float32) * (2.0 * math.pi / NSBIN)
    values = jnp.where(row <= half, jnp.cos(angles), jnp.sin(angles))
    return (values * (1.0 / math.sqrt(FEEDS))).astype(jnp.bfloat16)


def pack_body(range_ref, weight_ref, band_ref, out_ref):
    count = range_ref[1]
    params = [range_ref[0].astype(jnp.float32)]
    for m in range(MAXBIN):
        params.append(jnp.where(m < count, weight_ref[m], 0.0) * band_ref[...])
    slot = lax.broadcasted_iota(jnp.int32, (TILE, 128), 1) % 32 // OWNED
    for z in range(ZDIM):
        packed = jnp.zeros((TILE, 128), jnp.float32)
        for n, param in enumerate(params):
            moved = pltpu.roll(param, OWNED * (n - z) % 128, 1)
            packed = jnp.where(slot == n, moved, packed)
        out_ref[z] = packed


def pack(bin_range, weights, bandpass):
    return pl.pallas_call(
        pack_body,
        out_shape=jax.ShapeDtypeStruct((ZDIM, TILE, 128), jnp.float32),
        name="pack",
    )(bin_range, weights, bandpass.reshape(1, 128))


def grid_body(y_ref, *refs):
    pieces, out_ref = refs[:-1], refs[-1]
    y = y_ref[0]
    column = lax.broadcasted_iota(jnp.int32, (ZDIM * TILE, NSBIN), 1)
    bins = jnp.where(column <= NSBIN // 2, column, 3 * NSBIN // 2 - column)
    for shift, piece_ref in enumerate(pieces):
        source = lax.rem(y - shift + YDIM, YDIM)
        params = piece_ref[...].reshape(ZDIM * TILE, 128)
        params = pltpu.roll(params, lax.rem(128 - 32 * y, 128), 1)
        for ch in range(OWNED):
            offset = bins - params[:, ch : ch + 1].astype(jnp.int32)
            grid = jnp.zeros((ZDIM * TILE, NSBIN), jnp.float32)
            for m in range(MAXBIN):
                lane = OWNED * (m + 1) + ch
                grid = jnp.where(offset == m, params[:, lane : lane + 1], grid)
            high, low = split_bf16(grid)
            start = pl.multiple_of(ch * NSBEAM + source * ZDIM * TILE, ZDIM * TILE)
            out_ref[pl.ds(start, ZDIM * TILE), :NSBIN] = high
            out_ref[pl.ds(start, ZDIM * TILE), NSBIN:] = low


def regridding(y, pieces):
    return pl.pallas_call(
        grid_body,
        in_specs=[pl.BlockSpec(memory_space=pltpu.SMEM)]
        + [pl.BlockSpec(memory_space=pltpu.VMEM)] * len(pieces),
        out_specs=pl.BlockSpec(memory_space=pltpu.VMEM),
        out_shape=jax.ShapeDtypeStruct((OWNED * NSBEAM, 2 * NSBIN), jnp.bfloat16),
        compiler_params=pltpu.CompilerParams(vmem_limit_bytes=VMEM_LIMIT),
        cost_estimate=pl.CostEstimate(
            flops=10_000_000, bytes_accessed=2 * 2**20, transcendentals=0
        ),
        name="regridding",
    )(y, *pieces)


def east_west(x_ref, p):
    v = [x_ref[:, e * 32 + p * 16 : e * 32 + p * 16 + 16, :].astype(jnp.float32) for e in range(4)]
    re, im = [a[:, :TILE] for a in v], [a[:, TILE:] for a in v]
    even_re, odd_re, diff_re, turn_re = re[0] + re[2], re[1] + re[3], re[0] - re[2], re[1] - re[3]
    even_im, odd_im, diff_im, turn_im = im[0] + im[2], im[1] + im[3], im[0] - im[2], im[1] - im[3]
    real = (even_re + odd_re, diff_re + turn_im, even_re - odd_re, diff_re - turn_im)
    imag = (even_im + odd_im, diff_im - turn_re, even_im - odd_im, diff_im + turn_re)
    tidy = lambda beams: [beam.astype(jnp.bfloat16).reshape(FEEDS, 128) for beam in beams]
    return tidy(real), tidy(imag)


def squares(a, b):
    return a * a + b * b


def bin_power(table_ref, pols, k):
    (real0, imag0), (real1, imag1) = pols
    feeds = jnp.concatenate([real0[k], real1[k], imag0[k], imag1[k]], axis=1)
    sums = jnp.dot(table_ref[...], feeds, preferred_element_type=jnp.float32)
    half = NSBIN // 2
    cos_re, cos_im = sums[:half, :256], sums[:half, 256:]
    sin_re, sin_im = sums[half:, :256], sums[half:, 256:]
    plus = squares(cos_re + sin_im, cos_im - sin_re)
    minus = squares(cos_re - sin_im, cos_im + sin_re)
    top = lax.broadcasted_iota(jnp.int32, (TILE, 256), 0) == 0
    plus_top = jnp.where(top, squares(cos_re[:TILE], cos_im[:TILE]), plus[:TILE])
    minus_top = jnp.where(top, squares(sin_re[:TILE], sin_im[:TILE]), minus[:TILE])
    both = jnp.concatenate([plus_top, plus[TILE:], minus_top, minus[TILE:]], axis=0)
    return both[:, :128] + both[:, 128:]


def frame_sums(bins, channel):
    parts = [half for power in bins for half in split_bf16(power)]
    row = lax.broadcasted_iota(jnp.int32, (len(parts) * 128, 128), 0)
    lane = lax.broadcasted_iota(jnp.int32, (len(parts) * 128, 128), 1)
    target = channel * 32 + row % 128 // FLEN * 4 + row // 256
    summing = jnp.where(lane == target, 1.0 / (8.0 * FLEN), 0.0).astype(jnp.bfloat16)
    return jnp.dot(
        jnp.concatenate(parts, axis=1), summing, preferred_element_type=jnp.float32
    )


def beam_body(x_ref, grid_ref, table_ref, out_ref):
    power = jnp.zeros((NSBIN, 128), jnp.float32)
    for channel in range(OWNED):
        one = x_ref.at[:, channel * ROWS : (channel + 1) * ROWS]
        pols = [east_west(one, p) for p in range(2)]
        power += frame_sums([bin_power(table_ref, pols, k) for k in range(4)], channel)
    halves = jnp.concatenate(split_bf16(power), axis=1)
    beams = jnp.dot(
        grid_ref[...],
        jnp.concatenate([halves, halves], axis=0),
        preferred_element_type=jnp.float32,
    )
    beams = beams[:, :128] + beams[:, 128:]
    lane = lax.broadcasted_iota(jnp.int32, (NSBEAM, 128), 1) // 32
    out = beams[:NSBEAM]
    for channel in range(1, OWNED):
        out = jnp.where(lane == channel, beams[channel * NSBEAM : (channel + 1) * NSBEAM], out)
    out_ref[...] = out


def channel_beams(voltages, grid, table):
    return pl.pallas_call(
        beam_body,
        in_specs=[pl.BlockSpec(memory_space=pltpu.VMEM)] * 3,
        out_specs=pl.BlockSpec(memory_space=pltpu.VMEM),
        out_shape=jax.ShapeDtypeStruct((NSBEAM, 128), jnp.float32),
        compiler_params=pltpu.CompilerParams(vmem_limit_bytes=VMEM_LIMIT),
        cost_estimate=pl.CostEstimate(
            flops=3_000_000_000, bytes_accessed=6 * 2**20, transcendentals=0
        ),
        name="channel_beams",
    )(voltages, grid, table)


def flatten_body(beams_ref, sums_ref, out_ref):
    total = jnp.sum(sums_ref[...], axis=0)
    total = total + pltpu.roll(total, 64, 1)
    total = total + pltpu.roll(total, 32, 1)
    flat = beams_ref[...] / (total / CHANNELS + 1e-06)[None]
    lane = lax.broadcasted_iota(jnp.int32, (32, 128), 1) % OWNED
    for j in range(TILE):
        rows = flat[:, j, :]
        turned = jnp.repeat(rows, OWNED, axis=0).T
        picked = jnp.zeros((32, 128), jnp.float32)
        for ch in range(OWNED):
            picked = jnp.where(lane == ch, turned[ch * 32 : ch * 32 + 32], picked)
        out_ref[:, j, :] = picked


def flatten(beams, sums):
    return pl.pallas_call(
        flatten_body,
        out_shape=jax.ShapeDtypeStruct((32, TILE, 128), jnp.float32),
        name="flatten",
    )(beams, sums)


def shards(voltages, bin_range, weights, bandpass):
    columns = [[y * ZDIM + z for z in range(ZDIM)] for y in range(YDIM)]
    params = lax.all_to_all(
        pack(bin_range, weights, bandpass), "beam", 0, 0, axis_index_groups=columns, tiled=True
    )
    voltages, params = lax.optimization_barrier((voltages, params))
    volts = lax.all_to_all(
        voltages.reshape(PEERS, OWNED * ROWS, 128), "beam", 0, 0, tiled=True
    )
    pieces = [params] + [
        lax.ppermute(params, "beam", [(i, (i + shift * ZDIM) % PEERS) for i in range(PEERS)])
        for shift in range(1, YDIM)
    ]
    grid = regridding((lax.axis_index("beam") // ZDIM).reshape(1), pieces)
    beams = channel_beams(volts, grid, ns_table())
    beams = lax.all_to_all(beams.reshape(PEERS, TILE, 128), "beam", 0, 0, tiled=True)
    sums = jnp.broadcast_to(jnp.sum(beams, axis=0), (lax.axis_size("chan"), TILE, 128))
    sums = lax.all_to_all(sums, "chan", 0, 0, tiled=True)
    return flatten(beams, sums).reshape(8, 4, TILE, 128)


def solution(mesh):
    return jax.shard_map(
        shards,
        mesh=mesh,
        in_specs=(
            P("chan", None, None, None, "beam", None),
            P(None, "beam", "chan"),
            P(None, "beam", "chan"),
            P("chan"),
        ),
        out_specs=P(None, None, "beam", "chan"),
        check_vma=False,
    )
```

```python
import math

import jax
import jax.numpy as jnp
from jax import lax
from jax.experimental import pallas as pl
from jax.experimental.pallas import tpu as pltpu
from jax.sharding import PartitionSpec as P

CHANNELS = 1024
FEEDS = 256
NSBIN = 512
NSBEAM = 256
FLEN = 16
MAXBIN = 4
TILE = 8
YDIM, ZDIM = 4, 8
PEERS = YDIM * ZDIM
OWNED = 4
ROWS = 128
VMEM_LIMIT = 24 * 1024 * 1024
SMALL = pltpu.CompilerParams(vmem_limit_bytes=8 * 1024 * 1024)


def split_bf16(values):
    high = values.astype(jnp.bfloat16)
    low = (values - high.astype(jnp.float32)).astype(jnp.bfloat16)
    return high, low


def table_body(out_ref):
    row = lax.broadcasted_iota(jnp.int32, (NSBIN, FEEDS), 0)
    feed = lax.broadcasted_iota(jnp.int32, (NSBIN, FEEDS), 1)
    bins = row // 16 * 8 + row % 8
    middle = row == 8
    bins = jnp.where(middle, NSBIN // 2, bins)
    angles = (feed * bins % NSBIN).astype(jnp.float32) * (2.0 * math.pi / NSBIN)
    values = jnp.where(middle | (row % 16 < 8), jnp.cos(angles), jnp.sin(angles))
    out_ref[...] = (values * (1.0 / math.sqrt(FEEDS))).astype(jnp.bfloat16)


def ns_table():
    return pl.pallas_call(
        table_body,
        out_shape=jax.ShapeDtypeStruct((NSBIN, FEEDS), jnp.bfloat16),
        compiler_params=SMALL,
        name="ns_table",
    )()


def pack_body(range_ref, weight_ref, band_ref, out_ref):
    count = range_ref[1]
    params = [range_ref[0].astype(jnp.float32)]
    for m in range(MAXBIN):
        params.append(jnp.where(m < count, weight_ref[m], 0.0) * band_ref[...])
    slot = lax.broadcasted_iota(jnp.int32, (TILE, 128), 1) % 32 // OWNED
    for z in range(ZDIM):
        packed = jnp.zeros((TILE, 128), jnp.float32)
        for n, param in enumerate(params):
            moved = pltpu.roll(param, OWNED * (n - z) % 128, 1)
            packed = jnp.where(slot == n, moved, packed)
        out_ref[z] = packed


def pack(bin_range, weights, bandpass):
    return pl.pallas_call(
        pack_body,
        out_shape=jax.ShapeDtypeStruct((ZDIM, TILE, 128), jnp.float32),
        compiler_params=SMALL,
        name="pack",
    )(bin_range, weights, bandpass.reshape(1, 128))


def gather_body(*refs):
    pieces, outs = refs[:YDIM], refs[YDIM:]
    me = lax.axis_index("beam")
    y, z = me // ZDIM, lax.rem(me, ZDIM)
    lane = lax.broadcasted_iota(jnp.int32, (TILE, 128), 1) // 32
    for far, out_ref in enumerate(outs):
        target = lax.rem(z + far, ZDIM)
        merged = pieces[0][target]
        for shift in range(1, YDIM):
            moved = pltpu.roll(pieces[shift][target], 128 - 32 * shift, 1)
            merged = jnp.where(lane == lax.rem(y - shift + YDIM, YDIM), moved, merged)
        out_ref[...] = merged


def gather(pieces):
    return pl.pallas_call(
        gather_body,
        out_shape=[jax.ShapeDtypeStruct((TILE, 128), jnp.float32)] * ZDIM,
        compiler_params=SMALL,
        name="gather",
    )(*pieces)


def east_west(x_ref, p):
    v = [x_ref[:, e * 32 + p * 16 : e * 32 + p * 16 + 16, :].astype(jnp.float32) for e in range(4)]
    re, im = [a[:, :TILE] for a in v], [a[:, TILE:] for a in v]
    even_re, odd_re, diff_re, turn_re = re[0] + re[2], re[1] + re[3], re[0] - re[2], re[1] - re[3]
    even_im, odd_im, diff_im, turn_im = im[0] + im[2], im[1] + im[3], im[0] - im[2], im[1] - im[3]
    real = (even_re + odd_re, diff_re + turn_im, even_re - odd_re, diff_re - turn_im)
    imag = (even_im + odd_im, diff_im - turn_re, even_im - odd_im, diff_im + turn_re)
    tidy = lambda beams: [beam.astype(jnp.bfloat16).reshape(FEEDS, 128) for beam in beams]
    return tidy(real), tidy(imag)


def squares(a, b):
    return a * a + b * b


def bin_squares(sums):
    sums = sums.reshape(NSBIN // 16, 2, 8, 256)
    cos_re, cos_im = sums[:, 0, :, :128], sums[:, 0, :, 128:]
    sin_re, sin_im = sums[:, 1, :, :128], sums[:, 1, :, 128:]
    plus = squares(cos_re + sin_im, cos_im - sin_re)
    minus = squares(cos_re - sin_im, cos_im + sin_re)
    top = lax.broadcasted_iota(jnp.int32, (8, 128), 0) == 0
    plus_top = jnp.where(top, squares(cos_re[0], cos_im[0]), plus[0])[None]
    minus_top = jnp.where(top, squares(sin_re[0], sin_im[0]), minus[0])[None]
    return jnp.concatenate([plus_top, plus[1:], minus_top, minus[1:]], axis=0)


def bin_power(table_ref, pols, k):
    (real0, imag0), (real1, imag1) = pols
    feeds = jnp.concatenate([real0[k], imag0[k], real1[k], imag1[k]], axis=1)
    sums = jnp.dot(table_ref[...], feeds, preferred_element_type=jnp.float32)
    return (bin_squares(sums[:, :256]) + bin_squares(sums[:, 256:])).reshape(NSBIN, 128)


def frame_sums(bins, channel):
    parts = [half for power in bins for half in split_bf16(power)]
    row = lax.broadcasted_iota(jnp.int32, (len(parts) * 128, 128), 0)
    lane = lax.broadcasted_iota(jnp.int32, (len(parts) * 128, 128), 1)
    target = channel * 32 + row % 128 // FLEN * 4 + row // 256
    summing = jnp.where(lane == target, 1.0 / (8.0 * FLEN), 0.0).astype(jnp.bfloat16)
    return jnp.dot(
        jnp.concatenate(parts, axis=1), summing, preferred_element_type=jnp.float32
    )


def power_body(x_ref, table_ref, out_ref):
    power = jnp.zeros((NSBIN, 128), jnp.float32)
    for channel in range(OWNED):
        one = x_ref.at[:, channel * ROWS : (channel + 1) * ROWS]
        pols = [east_west(one, p) for p in range(2)]
        power += frame_sums([bin_power(table_ref, pols, k) for k in range(4)], channel)
    out_ref[...] = power


def channel_power(voltages, table):
    return pl.pallas_call(
        power_body,
        in_specs=[pl.BlockSpec(memory_space=pltpu.VMEM)] * 2,
        out_specs=pl.BlockSpec(memory_space=pltpu.VMEM),
        out_shape=jax.ShapeDtypeStruct((NSBIN, 128), jnp.float32),
        compiler_params=pltpu.CompilerParams(vmem_limit_bytes=VMEM_LIMIT),
        cost_estimate=pl.CostEstimate(
            flops=3_000_000_000, bytes_accessed=6 * 2**20, transcendentals=0
        ),
        name="channel_power",
    )(voltages, table)


def regrid_body(power_ref, *refs):
    pieces, out_ref, param_ref = refs[:ZDIM], refs[ZDIM], refs[ZDIM + 1]
    me = lax.axis_index("beam")
    for far, piece_ref in enumerate(pieces):
        param_ref[lax.rem(me - far + ZDIM, ZDIM)] = piece_ref[...]
    halves = jnp.concatenate(split_bf16(power_ref[...]), axis=1)
    halves = jnp.concatenate([halves, halves], axis=0)
    params = param_ref[...].reshape(ZDIM * TILE, 128)
    column = lax.broadcasted_iota(jnp.int32, (ZDIM * TILE, NSBIN), 1)
    bins = jnp.where(column <= NSBIN // 2, column, 3 * NSBIN // 2 - column)
    place = lax.broadcasted_iota(jnp.int32, (NSBEAM, 128), 1) // 32
    out = jnp.zeros((NSBEAM, 128), jnp.float32)
    for channel in range(OWNED):
        tiles = []
        for y in range(YDIM):
            lane = 32 * y + channel
            offset = bins - params[:, lane : lane + 1].astype(jnp.int32)
            grid = jnp.zeros((ZDIM * TILE, NSBIN), jnp.float32)
            for m in range(MAXBIN):
                lane += OWNED
                grid = jnp.where(offset == m, params[:, lane : lane + 1], grid)
            tiles.append(jnp.concatenate(split_bf16(grid), axis=1))
        beams = jnp.dot(
            jnp.concatenate(tiles, axis=0), halves, preferred_element_type=jnp.float32
        )
        out = jnp.where(place == channel, beams[:, :128] + beams[:, 128:], out)
    out_ref[...] = out


def regrid(power, pieces):
    return pl.pallas_call(
        regrid_body,
        out_shape=jax.ShapeDtypeStruct((NSBEAM, 128), jnp.float32),
        scratch_shapes=[pltpu.VMEM((ZDIM, TILE, 128), jnp.float32)],
        compiler_params=pltpu.CompilerParams(vmem_limit_bytes=VMEM_LIMIT),
        name="regrid",
    )(power, *pieces)


def flatten_body(beams_ref, sums_ref, out_ref):
    total = jnp.sum(sums_ref[...], axis=0)
    total = total + pltpu.roll(total, 64, 1)
    total = total + pltpu.roll(total, 32, 1)
    flat = beams_ref[...] / (total / CHANNELS + 1e-06)[None]
    lane = lax.broadcasted_iota(jnp.int32, (32, 128), 1) % OWNED
    for j in range(TILE):
        turned = jnp.repeat(flat[:, j, :], OWNED, axis=0).T
        picked = jnp.zeros((32, 128), jnp.float32)
        for ch in range(OWNED):
            picked = jnp.where(lane == ch, turned[ch * 32 : ch * 32 + 32], picked)
        out_ref[:, j, :] = picked


def flatten(beams, sums):
    return pl.pallas_call(
        flatten_body,
        out_shape=jax.ShapeDtypeStruct((32, TILE, 128), jnp.float32),
        compiler_params=SMALL,
        name="flatten",
    )(beams, sums)


def along_z(block, far):
    pairs = [
        (y * ZDIM + z, y * ZDIM + (z + far) % ZDIM) for y in range(YDIM) for z in range(ZDIM)
    ]
    return lax.ppermute(block, "beam", pairs)


def shards(voltages, bin_range, weights, bandpass):
    volts = lax.all_to_all(
        voltages.reshape(PEERS, OWNED * ROWS, 128), "beam", 0, 0, tiled=True
    )
    params = pack(bin_range, weights, bandpass)
    pieces = [params] + [
        lax.ppermute(params, "beam", [(i, (i + shift * ZDIM) % PEERS) for i in range(PEERS)])
        for shift in range(1, YDIM)
    ]
    pieces = list(gather(pieces))
    for far in range(2, ZDIM - 1):
        pieces[far] = along_z(pieces[far], far)
    volts, pieces[1], pieces[-1] = lax.optimization_barrier((volts, pieces[1], pieces[-1]))
    pieces[1] = along_z(pieces[1], 1)
    pieces[-1] = along_z(pieces[-1], ZDIM - 1)
    power = channel_power(volts, ns_table())
    beams = regrid(power, pieces)
    beams = lax.all_to_all(beams.reshape(PEERS, TILE, 128), "beam", 0, 0, tiled=True)
    sums = jnp.broadcast_to(jnp.sum(beams, axis=0), (lax.axis_size("chan"), TILE, 128))
    sums = lax.all_to_all(sums, "chan", 0, 0, tiled=True)
    return flatten(beams, sums).reshape(8, 4, TILE, 128)


def solution(mesh):
    return jax.shard_map(
        shards,
        mesh=mesh,
        in_specs=(
            P("chan", None, None, None, "beam", None),
            P(None, "beam", "chan"),
            P(None, "beam", "chan"),
            P("chan"),
        ),
        out_specs=P(None, None, "beam", "chan"),
        check_vma=False,
    )
```

```python
import math

import jax
import jax.numpy as jnp
from jax import lax
from jax.experimental import pallas as pl
from jax.experimental.pallas import tpu as pltpu
from jax.sharding import PartitionSpec as P

CHANNELS = 1024
FEEDS = 256
NSBIN = 512
NSBEAM = 256
FLEN = 16
MAXBIN = 4
TILE = 8
YDIM, ZDIM = 4, 8
PEERS = YDIM * ZDIM
SINGLES = (0, 3, 4, 5)
OWNED = 4
ROWS = 128
VMEM_LIMIT = 24 * 1024 * 1024
SMALL = pltpu.CompilerParams(vmem_limit_bytes=8 * 1024 * 1024)


def split_bf16(values):
    high = values.astype(jnp.bfloat16)
    low = (values - high.astype(jnp.float32)).astype(jnp.bfloat16)
    return high, low


def table_body(out_ref):
    row = lax.broadcasted_iota(jnp.int32, (NSBIN, FEEDS), 0)
    feed = lax.broadcasted_iota(jnp.int32, (NSBIN, FEEDS), 1)
    bins = row // 16 * 8 + row % 8
    middle = row == 8
    bins = jnp.where(middle, NSBIN // 2, bins)
    angles = (feed * bins % NSBIN).astype(jnp.float32) * (2.0 * math.pi / NSBIN)
    values = jnp.where(middle | (row % 16 < 8), jnp.cos(angles), jnp.sin(angles))
    out_ref[...] = (values * (1.0 / math.sqrt(FEEDS))).astype(jnp.bfloat16)


def ns_table():
    return pl.pallas_call(
        table_body,
        out_shape=jax.ShapeDtypeStruct((NSBIN, FEEDS), jnp.bfloat16),
        compiler_params=SMALL,
        name="ns_table",
    )()


def pack_body(range_ref, weight_ref, band_ref, out_ref):
    count = range_ref[1]
    params = [range_ref[0].astype(jnp.float32)]
    for m in range(MAXBIN):
        params.append(jnp.where(m < count, weight_ref[m], 0.0) * band_ref[...])
    slot = lax.broadcasted_iota(jnp.int32, (TILE, 128), 1) % 32 // OWNED
    for z in range(ZDIM):
        packed = jnp.zeros((TILE, 128), jnp.float32)
        for n, param in enumerate(params):
            moved = pltpu.roll(param, OWNED * (n - z) % 128, 1)
            packed = jnp.where(slot == n, moved, packed)
        out_ref[z] = packed


def pack(bin_range, weights, bandpass):
    return pl.pallas_call(
        pack_body,
        out_shape=jax.ShapeDtypeStruct((ZDIM, TILE, 128), jnp.float32),
        compiler_params=SMALL,
        name="pack",
    )(bin_range, weights, bandpass.reshape(1, 128))


def paired(core):
    return (
        (jnp.where(core == 0, 1, ZDIM - 1), jnp.where(core == 0, 2, ZDIM - 2)),
        (jnp.where(core == 0, ZDIM - 1, 1), jnp.where(core == 0, ZDIM - 2, 2)),
    )


def gather_body(*refs):
    pieces, (kept_ref, given_ref, *single_refs) = refs[:YDIM], refs[YDIM:]
    me = lax.axis_index("beam")
    y, z = me // ZDIM, lax.rem(me, ZDIM)
    lane = lax.broadcasted_iota(jnp.int32, (TILE, 128), 1) // 32

    def block(far):
        target = lax.rem(z + far, ZDIM)
        merged = pieces[0][target]
        for shift in range(1, YDIM):
            moved = pltpu.roll(pieces[shift][target], 128 - 32 * shift, 1)
            merged = jnp.where(lane == lax.rem(y - shift + YDIM, YDIM), moved, merged)
        return merged

    kept, given = paired(lax.rem(lax.axis_index("chan"), 2))
    for i in range(2):
        kept_ref[i] = block(kept[i])
        given_ref[i] = block(given[i])
    for far, single_ref in zip(SINGLES, single_refs):
        single_ref[...] = block(far)


def gather(pieces):
    single = jax.ShapeDtypeStruct((TILE, 128), jnp.float32)
    double = jax.ShapeDtypeStruct((2, TILE, 128), jnp.float32)
    return pl.pallas_call(
        gather_body,
        out_shape=[double] * 2 + [single] * len(SINGLES),
        compiler_params=SMALL,
        name="gather",
    )(*pieces)


def pair_body(kept_ref, got_ref, near_ref, far_ref):
    for i, out_ref in enumerate((near_ref, far_ref)):
        out_ref[0] = kept_ref[i]
        out_ref[1] = got_ref[i]


def pair(kept, got):
    return pl.pallas_call(
        pair_body,
        out_shape=[jax.ShapeDtypeStruct(kept.shape, jnp.float32)] * 2,
        compiler_params=SMALL,
        name="pair",
    )(kept, got)


def east_west(x_ref, p):
    v = [x_ref[:, e * 32 + p * 16 : e * 32 + p * 16 + 16, :].astype(jnp.float32) for e in range(4)]
    re, im = [a[:, :TILE] for a in v], [a[:, TILE:] for a in v]
    even_re, odd_re, diff_re, turn_re = re[0] + re[2], re[1] + re[3], re[0] - re[2], re[1] - re[3]
    even_im, odd_im, diff_im, turn_im = im[0] + im[2], im[1] + im[3], im[0] - im[2], im[1] - im[3]
    real = (even_re + odd_re, diff_re + turn_im, even_re - odd_re, diff_re - turn_im)
    imag = (even_im + odd_im, diff_im - turn_re, even_im - odd_im, diff_im + turn_re)
    tidy = lambda beams: [beam.astype(jnp.bfloat16).reshape(FEEDS, 128) for beam in beams]
    return tidy(real), tidy(imag)


def squares(a, b):
    return a * a + b * b


def bin_squares(sums):
    sums = sums.reshape(NSBIN // 16, 2, 8, 256)
    cos_re, cos_im = sums[:, 0, :, :128], sums[:, 0, :, 128:]
    sin_re, sin_im = sums[:, 1, :, :128], sums[:, 1, :, 128:]
    plus = squares(cos_re + sin_im, cos_im - sin_re)
    minus = squares(cos_re - sin_im, cos_im + sin_re)
    top = lax.broadcasted_iota(jnp.int32, (8, 128), 0) == 0
    plus_top = jnp.where(top, squares(cos_re[0], cos_im[0]), plus[0])[None]
    minus_top = jnp.where(top, squares(sin_re[0], sin_im[0]), minus[0])[None]
    return jnp.concatenate([plus_top, plus[1:], minus_top, minus[1:]], axis=0)


def bin_power(table_ref, pols, k):
    (real0, imag0), (real1, imag1) = pols
    feeds = jnp.concatenate([real0[k], imag0[k], real1[k], imag1[k]], axis=1)
    sums = jnp.dot(table_ref[...], feeds, preferred_element_type=jnp.float32)
    return (bin_squares(sums[:, :256]) + bin_squares(sums[:, 256:])).reshape(NSBIN, 128)


def frame_sums(bins, channel):
    parts = [half for power in bins for half in split_bf16(power)]
    row = lax.broadcasted_iota(jnp.int32, (len(parts) * 128, 128), 0)
    lane = lax.broadcasted_iota(jnp.int32, (len(parts) * 128, 128), 1)
    target = channel * 32 + row % 128 // FLEN * 4 + row // 256
    summing = jnp.where(lane == target, 1.0 / (8.0 * FLEN), 0.0).astype(jnp.bfloat16)
    return jnp.dot(
        jnp.concatenate(parts, axis=1), summing, preferred_element_type=jnp.float32
    )


def power_body(x_ref, table_ref, out_ref):
    power = jnp.zeros((NSBIN, 128), jnp.float32)
    for channel in range(OWNED):
        one = x_ref.at[:, channel * ROWS : (channel + 1) * ROWS]
        pols = [east_west(one, p) for p in range(2)]
        power += frame_sums([bin_power(table_ref, pols, k) for k in range(4)], channel)
    out_ref[...] = power


def channel_power(voltages, table):
    return pl.pallas_call(
        power_body,
        in_specs=[pl.BlockSpec(memory_space=pltpu.VMEM)] * 2,
        out_specs=pl.BlockSpec(memory_space=pltpu.VMEM),
        out_shape=jax.ShapeDtypeStruct((NSBIN, 128), jnp.float32),
        compiler_params=pltpu.CompilerParams(vmem_limit_bytes=VMEM_LIMIT),
        cost_estimate=pl.CostEstimate(
            flops=3_000_000_000, bytes_accessed=6 * 2**20, transcendentals=0
        ),
        name="channel_power",
    )(voltages, table)


def regrid_body(power_ref, *refs):
    near_ref, far_ref, near_swap_ref, far_swap_ref, *single_refs, out_ref, param_ref = refs
    z = lax.rem(lax.axis_index("beam"), ZDIM)
    kept, given = paired(lax.rem(lax.axis_index("chan"), 2))
    blocks = [(kept[0], near_ref[0]), (kept[1], far_ref[0])]
    blocks += [(given[0], near_swap_ref[1]), (given[1], far_swap_ref[1])]
    blocks += [(far, single_ref[...]) for far, single_ref in zip(SINGLES, single_refs)]
    for far, block in blocks:
        param_ref[lax.rem(z - far + ZDIM, ZDIM)] = block
    halves = jnp.concatenate(split_bf16(power_ref[...]), axis=1)
    halves = jnp.concatenate([halves, halves], axis=0)
    params = param_ref[...].reshape(ZDIM * TILE, 128)
    column = lax.broadcasted_iota(jnp.int32, (ZDIM * TILE, NSBIN), 1)
    bins = jnp.where(column <= NSBIN // 2, column, 3 * NSBIN // 2 - column)
    place = lax.broadcasted_iota(jnp.int32, (NSBEAM, 128), 1) // 32
    out = jnp.zeros((NSBEAM, 128), jnp.float32)
    for channel in range(OWNED):
        tiles = []
        for y in range(YDIM):
            lane = 32 * y + channel
            offset = bins - params[:, lane : lane + 1].astype(jnp.int32)
            grid = jnp.zeros((ZDIM * TILE, NSBIN), jnp.float32)
            for m in range(MAXBIN):
                lane += OWNED
                grid = jnp.where(offset == m, params[:, lane : lane + 1], grid)
            tiles.append(jnp.concatenate(split_bf16(grid), axis=1))
        beams = jnp.dot(
            jnp.concatenate(tiles, axis=0), halves, preferred_element_type=jnp.float32
        )
        out = jnp.where(place == channel, beams[:, :128] + beams[:, 128:], out)
    out_ref[...] = out


def regrid(power, pieces):
    return pl.pallas_call(
        regrid_body,
        out_shape=jax.ShapeDtypeStruct((NSBEAM, 128), jnp.float32),
        scratch_shapes=[pltpu.VMEM((ZDIM, TILE, 128), jnp.float32)],
        compiler_params=pltpu.CompilerParams(vmem_limit_bytes=VMEM_LIMIT),
        name="regrid",
    )(power, *pieces)


def flatten_body(beams_ref, sums_ref, out_ref):
    total = jnp.sum(sums_ref[...], axis=0)
    total = total + pltpu.roll(total, 64, 1)
    total = total + pltpu.roll(total, 32, 1)
    flat = beams_ref[...] / (total / CHANNELS + 1e-06)[None]
    lane = lax.broadcasted_iota(jnp.int32, (32, 128), 1) % OWNED
    for j in range(TILE):
        turned = jnp.repeat(flat[:, j, :], OWNED, axis=0).T
        picked = jnp.zeros((32, 128), jnp.float32)
        for ch in range(OWNED):
            picked = jnp.where(lane == ch, turned[ch * 32 : ch * 32 + 32], picked)
        out_ref[:, j, :] = picked


def flatten(beams, sums):
    return pl.pallas_call(
        flatten_body,
        out_shape=jax.ShapeDtypeStruct((32, TILE, 128), jnp.float32),
        compiler_params=SMALL,
        name="flatten",
    )(beams, sums)


def along_z(block, far):
    pairs = [
        (y * ZDIM + z, y * ZDIM + (z + far) % ZDIM) for y in range(YDIM) for z in range(ZDIM)
    ]
    return lax.ppermute(block, "beam", pairs)


def both_ways(block, far):
    pairs = []
    for g in range(lax.axis_size("chan")):
        for y in range(YDIM):
            for z in range(ZDIM):
                to = (z + far if g % 2 == 0 else z - far) % ZDIM
                pairs.append(((g * YDIM + y) * ZDIM + z, (g * YDIM + y) * ZDIM + to))
    return lax.ppermute(block, ("chan", "beam"), pairs)


def swap(block):
    return lax.ppermute(block, "chan", [(g, g ^ 1) for g in range(lax.axis_size("chan"))])


def shards(voltages, bin_range, weights, bandpass):
    volts = lax.all_to_all(
        voltages.reshape(PEERS, OWNED * ROWS, 128), "beam", 0, 0, tiled=True
    )
    params = pack(bin_range, weights, bandpass)
    pieces = [params] + [
        lax.ppermute(params, "beam", [(i, (i + shift * ZDIM) % PEERS) for i in range(PEERS)])
        for shift in range(1, YDIM)
    ]
    kept, given, *singles = gather(pieces)
    near, far = pair(kept, swap(given))
    near, far = both_ways(near, 1), both_ways(far, 2)
    singles[1:] = [along_z(single, dist) for single, dist in zip(singles[1:], SINGLES[1:])]
    volts, near, far = lax.optimization_barrier((volts, near, far))
    parts = [near, far, swap(near), swap(far)] + singles
    power = channel_power(volts, ns_table())
    beams = regrid(power, parts)
    beams = lax.all_to_all(beams.reshape(PEERS, TILE, 128), "beam", 0, 0, tiled=True)
    sums = jnp.broadcast_to(jnp.sum(beams, axis=0), (lax.axis_size("chan"), TILE, 128))
    sums = lax.all_to_all(sums, "chan", 0, 0, tiled=True)
    return flatten(beams, sums).reshape(8, 4, TILE, 128)


def solution(mesh):
    return jax.shard_map(
        shards,
        mesh=mesh,
        in_specs=(
            P("chan", None, None, None, "beam", None),
            P(None, "beam", "chan"),
            P(None, "beam", "chan"),
            P("chan"),
        ),
        out_specs=P(None, None, "beam", "chan"),
        check_vma=False,
    )
```

```python
import math

import jax
import jax.numpy as jnp
from jax import lax
from jax.experimental import pallas as pl
from jax.experimental.pallas import tpu as pltpu
from jax.sharding import PartitionSpec as P

CHANNELS = 1024
FEEDS = 256
NSBIN = 512
NSBEAM = 256
FLEN = 16
MAXBIN = 4
TILE = 8
YDIM, ZDIM = 4, 8
PEERS = YDIM * ZDIM
SINGLES = (0, 3, 4, 5)
OWNED = 4
ROWS = 128
VMEM_LIMIT = 24 * 1024 * 1024
SMALL = pltpu.CompilerParams(vmem_limit_bytes=8 * 1024 * 1024)


def split_bf16(values):
    high = values.astype(jnp.bfloat16)
    low = (values - high.astype(jnp.float32)).astype(jnp.bfloat16)
    return high, low


def table_body(out_ref):
    row = lax.broadcasted_iota(jnp.int32, (NSBIN, FEEDS), 0)
    feed = lax.broadcasted_iota(jnp.int32, (NSBIN, FEEDS), 1)
    bins = row // 16 * 8 + row % 8
    middle = row == 8
    bins = jnp.where(middle, NSBIN // 2, bins)
    angles = (feed * bins % NSBIN).astype(jnp.float32) * (2.0 * math.pi / NSBIN)
    values = jnp.where(middle | (row % 16 < 8), jnp.cos(angles), jnp.sin(angles))
    out_ref[...] = (values * (1.0 / math.sqrt(FEEDS))).astype(jnp.bfloat16)


def ns_table():
    return pl.pallas_call(
        table_body,
        out_shape=jax.ShapeDtypeStruct((NSBIN, FEEDS), jnp.bfloat16),
        compiler_params=SMALL,
        name="ns_table",
    )()


def pack_body(range_ref, weight_ref, band_ref, out_ref):
    count = range_ref[1]
    params = [range_ref[0].astype(jnp.float32)]
    for m in range(MAXBIN):
        params.append(jnp.where(m < count, weight_ref[m], 0.0) * band_ref[...])
    slot = lax.broadcasted_iota(jnp.int32, (TILE, 128), 1) % 32 // OWNED
    for z in range(ZDIM):
        packed = jnp.zeros((TILE, 128), jnp.float32)
        for n, param in enumerate(params):
            moved = pltpu.roll(param, OWNED * (n - z) % 128, 1)
            packed = jnp.where(slot == n, moved, packed)
        out_ref[z] = packed


def pack(bin_range, weights, bandpass):
    return pl.pallas_call(
        pack_body,
        out_shape=jax.ShapeDtypeStruct((ZDIM, TILE, 128), jnp.float32),
        compiler_params=SMALL,
        name="pack",
    )(bin_range, weights, bandpass.reshape(1, 128))


def paired(core):
    return (
        (jnp.where(core == 0, 1, ZDIM - 1), jnp.where(core == 0, 2, ZDIM - 2)),
        (jnp.where(core == 0, ZDIM - 1, 1), jnp.where(core == 0, ZDIM - 2, 2)),
    )


def gather_body(*refs):
    pieces, (kept_ref, given_ref, *single_refs) = refs[:YDIM], refs[YDIM:]
    me = lax.axis_index("beam")
    y, z = me // ZDIM, lax.rem(me, ZDIM)
    lane = lax.broadcasted_iota(jnp.int32, (TILE, 128), 1) // 32

    def block(far):
        target = lax.rem(z + far, ZDIM)
        merged = pieces[0][target]
        for shift in range(1, YDIM):
            moved = pltpu.roll(pieces[shift][target], 128 - 32 * shift, 1)
            merged = jnp.where(lane == lax.rem(y - shift + YDIM, YDIM), moved, merged)
        return merged

    kept, given = paired(lax.rem(lax.axis_index("chan"), 2))
    for i in range(2):
        kept_ref[i] = block(kept[i])
        given_ref[i] = block(given[i])
    for far, single_ref in zip(SINGLES, single_refs):
        single_ref[...] = block(far)


def gather(pieces):
    single = jax.ShapeDtypeStruct((TILE, 128), jnp.float32)
    double = jax.ShapeDtypeStruct((2, TILE, 128), jnp.float32)
    return pl.pallas_call(
        gather_body,
        out_shape=[double] * 2 + [single] * len(SINGLES),
        compiler_params=SMALL,
        name="gather",
    )(*pieces)


def pair_body(kept_ref, got_ref, near_ref, far_ref):
    for i, out_ref in enumerate((near_ref, far_ref)):
        out_ref[0] = kept_ref[i]
        out_ref[1] = got_ref[i]


def pair(kept, got):
    return pl.pallas_call(
        pair_body,
        out_shape=[jax.ShapeDtypeStruct(kept.shape, jnp.float32)] * 2,
        compiler_params=SMALL,
        name="pair",
    )(kept, got)


def east_west(x_ref, p):
    v = [x_ref[:, e * 32 + p * 16 : e * 32 + p * 16 + 16, :].astype(jnp.float32) for e in range(4)]
    re, im = [a[:, :TILE] for a in v], [a[:, TILE:] for a in v]
    even_re, odd_re, diff_re, turn_re = re[0] + re[2], re[1] + re[3], re[0] - re[2], re[1] - re[3]
    even_im, odd_im, diff_im, turn_im = im[0] + im[2], im[1] + im[3], im[0] - im[2], im[1] - im[3]
    real = (even_re + odd_re, diff_re + turn_im, even_re - odd_re, diff_re - turn_im)
    imag = (even_im + odd_im, diff_im - turn_re, even_im - odd_im, diff_im + turn_re)
    tidy = lambda beams: [beam.astype(jnp.bfloat16).reshape(FEEDS, 128) for beam in beams]
    return tidy(real), tidy(imag)


def squares(a, b):
    return a * a + b * b


def bin_squares(sums):
    sums = sums.reshape(NSBIN // 16, 2, 8, 256)
    cos_re, cos_im = sums[:, 0, :, :128], sums[:, 0, :, 128:]
    sin_re, sin_im = sums[:, 1, :, :128], sums[:, 1, :, 128:]
    plus = squares(cos_re + sin_im, cos_im - sin_re)
    minus = squares(cos_re - sin_im, cos_im + sin_re)
    top = lax.broadcasted_iota(jnp.int32, (8, 128), 0) == 0
    plus_top = jnp.where(top, squares(cos_re[0], cos_im[0]), plus[0])[None]
    minus_top = jnp.where(top, squares(sin_re[0], sin_im[0]), minus[0])[None]
    return jnp.concatenate([plus_top, plus[1:], minus_top, minus[1:]], axis=0)


def bin_power(table_ref, pols, k):
    (real0, imag0), (real1, imag1) = pols
    feeds = jnp.concatenate([real0[k], imag0[k], real1[k], imag1[k]], axis=1)
    sums = jnp.dot(table_ref[...], feeds, preferred_element_type=jnp.float32)
    return (bin_squares(sums[:, :256]) + bin_squares(sums[:, 256:])).reshape(NSBIN, 128)


def frame_sums(bins, channel):
    parts = [half for power in bins for half in split_bf16(power)]
    row = lax.broadcasted_iota(jnp.int32, (len(parts) * 128, 128), 0)
    lane = lax.broadcasted_iota(jnp.int32, (len(parts) * 128, 128), 1)
    target = channel * 32 + row % 128 // FLEN * 4 + row // 256
    summing = jnp.where(lane == target, 1.0 / (8.0 * FLEN), 0.0).astype(jnp.bfloat16)
    return jnp.dot(
        jnp.concatenate(parts, axis=1), summing, preferred_element_type=jnp.float32
    )


def power_body(x_ref, table_ref, out_ref):
    power = jnp.zeros((NSBIN, 128), jnp.float32)
    for channel in range(OWNED):
        one = x_ref.at[:, channel * ROWS : (channel + 1) * ROWS]
        pols = [east_west(one, p) for p in range(2)]
        power += frame_sums([bin_power(table_ref, pols, k) for k in range(4)], channel)
    out_ref[...] = power


def channel_power(voltages, table):
    return pl.pallas_call(
        power_body,
        in_specs=[pl.BlockSpec(memory_space=pltpu.VMEM)] * 2,
        out_specs=pl.BlockSpec(memory_space=pltpu.VMEM),
        out_shape=jax.ShapeDtypeStruct((NSBIN, 128), jnp.float32),
        compiler_params=pltpu.CompilerParams(vmem_limit_bytes=VMEM_LIMIT),
        cost_estimate=pl.CostEstimate(
            flops=3_000_000_000, bytes_accessed=6 * 2**20, transcendentals=0
        ),
        name="channel_power",
    )(voltages, table)


def regrid_body(power_ref, *refs):
    near_ref, far_ref, near_swap_ref, far_swap_ref, *single_refs, out_ref, param_ref = refs
    z = lax.rem(lax.axis_index("beam"), ZDIM)
    kept, given = paired(lax.rem(lax.axis_index("chan"), 2))
    blocks = [(kept[0], near_ref[0]), (kept[1], far_ref[0])]
    blocks += [(given[0], near_swap_ref[1]), (given[1], far_swap_ref[1])]
    blocks += [(far, single_ref[...]) for far, single_ref in zip(SINGLES, single_refs)]
    for far, block in blocks:
        param_ref[lax.rem(z - far + ZDIM, ZDIM)] = block
    halves = jnp.concatenate(split_bf16(power_ref[...]), axis=1)
    halves = jnp.concatenate([halves, halves], axis=0)
    params = param_ref[...].reshape(ZDIM * TILE, 128)
    column = lax.broadcasted_iota(jnp.int32, (ZDIM * TILE, NSBIN), 1)
    bins = jnp.where(column <= NSBIN // 2, column, 3 * NSBIN // 2 - column)
    place = lax.broadcasted_iota(jnp.int32, (NSBEAM, 128), 1) // 32
    out = jnp.zeros((NSBEAM, 128), jnp.float32)
    for channel in range(OWNED):
        tiles = []
        for y in range(YDIM):
            lane = 32 * y + channel
            offset = bins - params[:, lane : lane + 1].astype(jnp.int32)
            grid = jnp.zeros((ZDIM * TILE, NSBIN), jnp.float32)
            for m in range(MAXBIN):
                lane += OWNED
                grid = jnp.where(offset == m, params[:, lane : lane + 1], grid)
            tiles.append(jnp.concatenate(split_bf16(grid), axis=1))
        beams = jnp.dot(
            jnp.concatenate(tiles, axis=0), halves, preferred_element_type=jnp.float32
        )
        out = jnp.where(place == channel, beams[:, :128] + beams[:, 128:], out)
    for y in range(YDIM):
        for z in range(ZDIM):
            row = (y * ZDIM + z) * TILE
            out_ref[z * YDIM + y] = out[row : row + TILE]


def regrid(power, pieces):
    return pl.pallas_call(
        regrid_body,
        out_shape=jax.ShapeDtypeStruct((PEERS, TILE, 128), jnp.float32),
        scratch_shapes=[pltpu.VMEM((ZDIM, TILE, 128), jnp.float32)],
        compiler_params=pltpu.CompilerParams(vmem_limit_bytes=VMEM_LIMIT),
        name="regrid",
    )(power, *pieces)


def flatten_body(beams_ref, sums_ref, out_ref):
    total = jnp.sum(sums_ref[...], axis=0)
    total = total + pltpu.roll(total, 64, 1)
    total = total + pltpu.roll(total, 32, 1)
    flat = beams_ref[...] / (total / CHANNELS + 1e-06)[None]
    flat = jnp.stack([flat[z * YDIM + y] for y in range(YDIM) for z in range(ZDIM)])
    lane = lax.broadcasted_iota(jnp.int32, (32, 128), 1) % OWNED
    for j in range(TILE):
        turned = jnp.repeat(flat[:, j, :], OWNED, axis=0).T
        picked = jnp.zeros((32, 128), jnp.float32)
        for ch in range(OWNED):
            picked = jnp.where(lane == ch, turned[ch * 32 : ch * 32 + 32], picked)
        out_ref[:, j, :] = picked


def flatten(beams, sums):
    return pl.pallas_call(
        flatten_body,
        out_shape=jax.ShapeDtypeStruct((32, TILE, 128), jnp.float32),
        compiler_params=SMALL,
        name="flatten",
    )(beams, sums)


def along_z(block, far):
    pairs = [
        (y * ZDIM + z, y * ZDIM + (z + far) % ZDIM) for y in range(YDIM) for z in range(ZDIM)
    ]
    return lax.ppermute(block, "beam", pairs)


def both_ways(block, far):
    pairs = []
    for g in range(lax.axis_size("chan")):
        for y in range(YDIM):
            for z in range(ZDIM):
                to = (z + far if g % 2 == 0 else z - far) % ZDIM
                pairs.append(((g * YDIM + y) * ZDIM + z, (g * YDIM + y) * ZDIM + to))
    return lax.ppermute(block, ("chan", "beam"), pairs)


def swap(block):
    return lax.ppermute(block, "chan", [(g, g ^ 1) for g in range(lax.axis_size("chan"))])


def shards(voltages, bin_range, weights, bandpass):
    volts = lax.all_to_all(
        voltages.reshape(PEERS, OWNED * ROWS, 128), "beam", 0, 0, tiled=True
    )
    params = pack(bin_range, weights, bandpass)
    pieces = [params] + [
        lax.ppermute(params, "beam", [(i, (i + shift * ZDIM) % PEERS) for i in range(PEERS)])
        for shift in range(1, YDIM)
    ]
    kept, given, *singles = gather(pieces)
    near, far = pair(kept, swap(given))
    near, far = both_ways(near, 1), both_ways(far, 2)
    singles[1:] = [along_z(single, dist) for single, dist in zip(singles[1:], SINGLES[1:])]
    volts, near, far = lax.optimization_barrier((volts, near, far))
    parts = [near, far, swap(near), swap(far)] + singles
    power = channel_power(volts, ns_table())
    beams = regrid(power, parts)
    z_first = [[y * ZDIM + z for z in range(ZDIM) for y in range(YDIM)]]
    beams = lax.all_to_all(beams, "beam", 0, 0, axis_index_groups=z_first, tiled=True)
    sums = jnp.broadcast_to(jnp.sum(beams, axis=0), (lax.axis_size("chan"), TILE, 128))
    sums = lax.all_to_all(sums, "chan", 0, 0, tiled=True)
    return flatten(beams, sums).reshape(8, 4, TILE, 128)


def solution(mesh):
    return jax.shard_map(
        shards,
        mesh=mesh,
        in_specs=(
            P("chan", None, None, None, "beam", None),
            P(None, "beam", "chan"),
            P(None, "beam", "chan"),
            P("chan"),
        ),
        out_specs=P(None, None, "beam", "chan"),
        check_vma=False,
    )
```

```python
import math

import jax
import jax.numpy as jnp
from jax import lax
from jax.experimental import pallas as pl
from jax.experimental.pallas import tpu as pltpu
from jax.sharding import PartitionSpec as P

CHANNELS = 1024
FEEDS = 256
NSBIN = 512
NSBEAM = 256
FLEN = 16
MAXBIN = 4
TILE = 8
YDIM, ZDIM = 4, 8
PEERS = YDIM * ZDIM
SINGLES = (0, 3, 4, 5)
OWNED = 4
ROWS = 128
VMEM_LIMIT = 24 * 1024 * 1024
SMALL = pltpu.CompilerParams(vmem_limit_bytes=8 * 1024 * 1024)


def split_bf16(values):
    high = values.astype(jnp.bfloat16)
    low = (values - high.astype(jnp.float32)).astype(jnp.bfloat16)
    return high, low


def table_body(out_ref):
    row = lax.broadcasted_iota(jnp.int32, (NSBIN, FEEDS), 0)
    feed = lax.broadcasted_iota(jnp.int32, (NSBIN, FEEDS), 1)
    bins = row // 16 * 8 + row % 8
    middle = row == 8
    bins = jnp.where(middle, NSBIN // 2, bins)
    angles = (feed * bins % NSBIN).astype(jnp.float32) * (2.0 * math.pi / NSBIN)
    values = jnp.where(middle | (row % 16 < 8), jnp.cos(angles), jnp.sin(angles))
    out_ref[...] = (values * (1.0 / math.sqrt(FEEDS))).astype(jnp.bfloat16)


def ns_table():
    return pl.pallas_call(
        table_body,
        out_shape=jax.ShapeDtypeStruct((NSBIN, FEEDS), jnp.bfloat16),
        compiler_params=SMALL,
        name="ns_table",
    )()


def pack_body(range_ref, weight_ref, band_ref, out_ref):
    count = range_ref[1]
    params = [range_ref[0].astype(jnp.float32)]
    for m in range(MAXBIN):
        params.append(jnp.where(m < count, weight_ref[m], 0.0) * band_ref[...])
    slot = lax.broadcasted_iota(jnp.int32, (TILE, 128), 1) % 32 // OWNED
    for z in range(ZDIM):
        packed = jnp.zeros((TILE, 128), jnp.float32)
        for n, param in enumerate(params):
            moved = pltpu.roll(param, OWNED * (n - z) % 128, 1)
            packed = jnp.where(slot == n, moved, packed)
        out_ref[z] = packed


def pack(bin_range, weights, bandpass):
    return pl.pallas_call(
        pack_body,
        out_shape=jax.ShapeDtypeStruct((ZDIM, TILE, 128), jnp.float32),
        compiler_params=SMALL,
        name="pack",
    )(bin_range, weights, bandpass.reshape(1, 128))


def paired(core):
    return (
        (jnp.where(core == 0, 1, ZDIM - 1), jnp.where(core == 0, 2, ZDIM - 2)),
        (jnp.where(core == 0, ZDIM - 1, 1), jnp.where(core == 0, ZDIM - 2, 2)),
    )


def gather_body(*refs):
    pieces, (kept_ref, given_ref, *single_refs) = refs[:YDIM], refs[YDIM:]
    me = lax.axis_index("beam")
    y, z = me // ZDIM, lax.rem(me, ZDIM)
    lane = lax.broadcasted_iota(jnp.int32, (TILE, 128), 1) // 32

    def block(far):
        target = lax.rem(z + far, ZDIM)
        merged = pieces[0][target]
        for shift in range(1, YDIM):
            moved = pltpu.roll(pieces[shift][target], 128 - 32 * shift, 1)
            merged = jnp.where(lane == lax.rem(y - shift + YDIM, YDIM), moved, merged)
        return merged

    kept, given = paired(lax.rem(lax.axis_index("chan"), 2))
    for i in range(2):
        kept_ref[i] = block(kept[i])
        given_ref[i] = block(given[i])
    for far, single_ref in zip(SINGLES, single_refs):
        single_ref[...] = block(far)


def gather(pieces):
    single = jax.ShapeDtypeStruct((TILE, 128), jnp.float32)
    double = jax.ShapeDtypeStruct((2, TILE, 128), jnp.float32)
    return pl.pallas_call(
        gather_body,
        out_shape=[double] * 2 + [single] * len(SINGLES),
        compiler_params=SMALL,
        name="gather",
    )(*pieces)


def pair_body(kept_ref, got_ref, near_ref, far_ref):
    for i, out_ref in enumerate((near_ref, far_ref)):
        out_ref[0] = kept_ref[i]
        out_ref[1] = got_ref[i]


def pair(kept, got):
    return pl.pallas_call(
        pair_body,
        out_shape=[jax.ShapeDtypeStruct(kept.shape, jnp.float32)] * 2,
        compiler_params=SMALL,
        name="pair",
    )(kept, got)


def east_west(x_ref, p):
    v = [x_ref[:, e * 32 + p * 16 : e * 32 + p * 16 + 16, :].astype(jnp.float32) for e in range(4)]
    re, im = [a[:, :TILE] for a in v], [a[:, TILE:] for a in v]
    even_re, odd_re, diff_re, turn_re = re[0] + re[2], re[1] + re[3], re[0] - re[2], re[1] - re[3]
    even_im, odd_im, diff_im, turn_im = im[0] + im[2], im[1] + im[3], im[0] - im[2], im[1] - im[3]
    real = (even_re + odd_re, diff_re + turn_im, even_re - odd_re, diff_re - turn_im)
    imag = (even_im + odd_im, diff_im - turn_re, even_im - odd_im, diff_im + turn_re)
    tidy = lambda beams: [beam.astype(jnp.bfloat16).reshape(FEEDS, 128) for beam in beams]
    return tidy(real), tidy(imag)


def squares(a, b):
    return a * a + b * b


def bin_squares(sums):
    sums = sums.reshape(NSBIN // 16, 2, 8, 256)
    cos_re, cos_im = sums[:, 0, :, :128], sums[:, 0, :, 128:]
    sin_re, sin_im = sums[:, 1, :, :128], sums[:, 1, :, 128:]
    plus = squares(cos_re + sin_im, cos_im - sin_re)
    minus = squares(cos_re - sin_im, cos_im + sin_re)
    top = lax.broadcasted_iota(jnp.int32, (8, 128), 0) == 0
    plus_top = jnp.where(top, squares(cos_re[0], cos_im[0]), plus[0])[None]
    minus_top = jnp.where(top, squares(sin_re[0], sin_im[0]), minus[0])[None]
    return jnp.concatenate([plus_top, plus[1:], minus_top, minus[1:]], axis=0)


def bin_power(table_ref, pols, k):
    (real0, imag0), (real1, imag1) = pols
    feeds = jnp.concatenate([real0[k], imag0[k], real1[k], imag1[k]], axis=1)
    sums = jnp.dot(table_ref[...], feeds, preferred_element_type=jnp.float32)
    return (bin_squares(sums[:, :256]) + bin_squares(sums[:, 256:])).reshape(NSBIN, 128)


def frame_sums(bins, channel):
    parts = [half for power in bins for half in split_bf16(power)]
    row = lax.broadcasted_iota(jnp.int32, (len(parts) * 128, 128), 0)
    lane = lax.broadcasted_iota(jnp.int32, (len(parts) * 128, 128), 1)
    target = channel * 32 + row % 128 // FLEN * 4 + row // 256
    summing = jnp.where(lane == target, 1.0 / (8.0 * FLEN), 0.0).astype(jnp.bfloat16)
    return jnp.dot(
        jnp.concatenate(parts, axis=1), summing, preferred_element_type=jnp.float32
    )


def power_body(x_ref, table_ref, out_ref):
    power = jnp.zeros((NSBIN, 128), jnp.float32)
    for channel in range(OWNED):
        one = x_ref.at[:, channel * ROWS : (channel + 1) * ROWS]
        pols = [east_west(one, p) for p in range(2)]
        power += frame_sums([bin_power(table_ref, pols, k) for k in range(4)], channel)
    out_ref[...] = power


def channel_power(voltages, table):
    return pl.pallas_call(
        power_body,
        in_specs=[pl.BlockSpec(memory_space=pltpu.VMEM)] * 2,
        out_specs=pl.BlockSpec(memory_space=pltpu.VMEM),
        out_shape=jax.ShapeDtypeStruct((NSBIN, 128), jnp.float32),
        compiler_params=pltpu.CompilerParams(vmem_limit_bytes=VMEM_LIMIT),
        cost_estimate=pl.CostEstimate(
            flops=3_000_000_000, bytes_accessed=6 * 2**20, transcendentals=0
        ),
        name="channel_power",
    )(voltages, table)


def regrid_body(power_ref, *refs):
    near_ref, far_ref, near_swap_ref, far_swap_ref, *single_refs, out_ref, param_ref = refs
    z = lax.rem(lax.axis_index("beam"), ZDIM)
    kept, given = paired(lax.rem(lax.axis_index("chan"), 2))
    blocks = [(kept[0], near_ref[0]), (kept[1], far_ref[0])]
    blocks += [(given[0], near_swap_ref[1]), (given[1], far_swap_ref[1])]
    blocks += [(far, single_ref[...]) for far, single_ref in zip(SINGLES, single_refs)]
    for far, block in blocks:
        param_ref[lax.rem(z - far + ZDIM, ZDIM)] = block
    halves = jnp.concatenate(split_bf16(power_ref[...]), axis=1)
    halves = jnp.concatenate([halves, halves], axis=0)
    params = param_ref[...].reshape(ZDIM * TILE, 128)
    column = lax.broadcasted_iota(jnp.int32, (ZDIM * TILE, NSBIN), 1)
    bins = jnp.where(column <= NSBIN // 2, column, 3 * NSBIN // 2 - column)
    place = lax.broadcasted_iota(jnp.int32, (NSBEAM, 128), 1) // 32
    out = jnp.zeros((NSBEAM, 128), jnp.float32)
    for channel in range(OWNED):
        tiles = []
        for y in range(YDIM):
            lane = 32 * y + channel
            offset = bins - params[:, lane : lane + 1].astype(jnp.int32)
            grid = jnp.zeros((ZDIM * TILE, NSBIN), jnp.float32)
            for m in range(MAXBIN):
                lane += OWNED
                grid = jnp.where(offset == m, params[:, lane : lane + 1], grid)
            tiles.append(jnp.concatenate(split_bf16(grid), axis=1))
        beams = jnp.dot(
            jnp.concatenate(tiles, axis=0), halves, preferred_element_type=jnp.float32
        )
        out = jnp.where(place == channel, beams[:, :128] + beams[:, 128:], out)
    out_ref[...] = out


def regrid(power, pieces):
    return pl.pallas_call(
        regrid_body,
        out_shape=jax.ShapeDtypeStruct((NSBEAM, 128), jnp.float32),
        scratch_shapes=[pltpu.VMEM((ZDIM, TILE, 128), jnp.float32)],
        compiler_params=pltpu.CompilerParams(vmem_limit_bytes=VMEM_LIMIT),
        name="regrid",
    )(power, *pieces)


def flatten_body(beams_ref, sums_ref, out_ref):
    total = jnp.sum(sums_ref[...], axis=0)
    total = total + pltpu.roll(total, 64, 1)
    total = total + pltpu.roll(total, 32, 1)
    flat = beams_ref[...] / (total / CHANNELS + 1e-06)[None]
    lane = lax.broadcasted_iota(jnp.int32, (32, 128), 1) % OWNED
    for j in range(TILE):
        turned = jnp.repeat(flat[:, j, :], OWNED, axis=0).T
        picked = jnp.zeros((32, 128), jnp.float32)
        for ch in range(OWNED):
            picked = jnp.where(lane == ch, turned[ch * 32 : ch * 32 + 32], picked)
        out_ref[:, j, :] = picked


def flatten(beams, sums):
    return pl.pallas_call(
        flatten_body,
        out_shape=jax.ShapeDtypeStruct((32, TILE, 128), jnp.float32),
        compiler_params=SMALL,
        name="flatten",
    )(beams, sums)


def along_z(block, far):
    pairs = [
        (y * ZDIM + z, y * ZDIM + (z + far) % ZDIM) for y in range(YDIM) for z in range(ZDIM)
    ]
    return lax.ppermute(block, "beam", pairs)


def both_ways(block, far):
    pairs = []
    for g in range(lax.axis_size("chan")):
        for y in range(YDIM):
            for z in range(ZDIM):
                to = (z + far if g % 2 == 0 else z - far) % ZDIM
                pairs.append(((g * YDIM + y) * ZDIM + z, (g * YDIM + y) * ZDIM + to))
    return lax.ppermute(block, ("chan", "beam"), pairs)


def swap(block):
    return lax.ppermute(block, "chan", [(g, g ^ 1) for g in range(lax.axis_size("chan"))])


def shards(voltages, bin_range, weights, bandpass):
    volts = lax.all_to_all(
        voltages.reshape(PEERS, OWNED * ROWS, 128), "beam", 0, 0, tiled=True
    )
    params = pack(bin_range, weights, bandpass)
    pieces = [params] + [
        lax.ppermute(params, "beam", [(i, (i + shift * ZDIM) % PEERS) for i in range(PEERS)])
        for shift in range(1, YDIM)
    ]
    kept, given, *singles = gather(pieces)
    near, far = pair(kept, swap(given))
    near, far = both_ways(near, 1), both_ways(far, 2)
    singles[1:] = [along_z(single, dist) for single, dist in zip(singles[1:], SINGLES[1:])]
    volts, near, far = lax.optimization_barrier((volts, near, far))
    parts = [near, far, swap(near), swap(far)] + singles
    power = channel_power(volts, ns_table())
    beams = regrid(power, parts)
    beams = lax.all_to_all(beams.reshape(PEERS, TILE, 128), "beam", 0, 0, tiled=True)
    sums = jnp.broadcast_to(jnp.sum(beams, axis=0), (lax.axis_size("chan"), TILE, 128))
    size = lax.axis_size("chan")
    core_first = [[*range(0, size, 2), *range(1, size, 2)]]
    sums = lax.all_to_all(sums, "chan", 0, 0, axis_index_groups=core_first, tiled=True)
    return flatten(beams, sums).reshape(8, 4, TILE, 128)


def solution(mesh):
    return jax.shard_map(
        shards,
        mesh=mesh,
        in_specs=(
            P("chan", None, None, None, "beam", None),
            P(None, "beam", "chan"),
            P(None, "beam", "chan"),
            P("chan"),
        ),
        out_specs=P(None, None, "beam", "chan"),
        check_vma=False,
    )
```

```python
import math

import jax
import jax.numpy as jnp
from jax import lax
from jax.experimental import pallas as pl
from jax.experimental.pallas import tpu as pltpu
from jax.sharding import PartitionSpec as P

CHANNELS = 1024
FEEDS = 256
NSBIN = 512
NSBEAM = 256
FLEN = 16
MAXBIN = 4
TILE = 8
YDIM, ZDIM = 4, 8
PEERS = YDIM * ZDIM
SINGLES = (0, 3, 4, 5)
OWNED = 4
ROWS = 128
VMEM_LIMIT = 24 * 1024 * 1024
SMALL = pltpu.CompilerParams(vmem_limit_bytes=8 * 1024 * 1024)


def split_bf16(values):
    high = values.astype(jnp.bfloat16)
    low = (values - high.astype(jnp.float32)).astype(jnp.bfloat16)
    return high, low


def table_body(out_ref):
    row = lax.broadcasted_iota(jnp.int32, (NSBIN, FEEDS), 0)
    feed = lax.broadcasted_iota(jnp.int32, (NSBIN, FEEDS), 1)
    bins = row // 16 * 8 + row % 8
    middle = row == 8
    bins = jnp.where(middle, NSBIN // 2, bins)
    angles = (feed * bins % NSBIN).astype(jnp.float32) * (2.0 * math.pi / NSBIN)
    values = jnp.where(middle | (row % 16 < 8), jnp.cos(angles), jnp.sin(angles))
    out_ref[...] = (values * (1.0 / math.sqrt(FEEDS))).astype(jnp.bfloat16)


def ns_table():
    return pl.pallas_call(
        table_body,
        out_shape=jax.ShapeDtypeStruct((NSBIN, FEEDS), jnp.bfloat16),
        compiler_params=SMALL,
        name="ns_table",
    )()


def pack_body(range_ref, weight_ref, band_ref, out_ref):
    count = range_ref[1]
    params = [range_ref[0].astype(jnp.float32)]
    for m in range(MAXBIN):
        params.append(jnp.where(m < count, weight_ref[m], 0.0) * band_ref[...])
    slot = lax.broadcasted_iota(jnp.int32, (TILE, 128), 1) % 32 // OWNED
    for z in range(ZDIM):
        packed = jnp.zeros((TILE, 128), jnp.float32)
        for n, param in enumerate(params):
            moved = pltpu.roll(param, OWNED * (n - z) % 128, 1)
            packed = jnp.where(slot == n, moved, packed)
        out_ref[z] = packed


def pack(bin_range, weights, bandpass):
    return pl.pallas_call(
        pack_body,
        out_shape=jax.ShapeDtypeStruct((ZDIM, TILE, 128), jnp.float32),
        compiler_params=SMALL,
        name="pack",
    )(bin_range, weights, bandpass.reshape(1, 128))


def paired(core):
    return (
        (jnp.where(core == 0, 1, ZDIM - 1), jnp.where(core == 0, 2, ZDIM - 2)),
        (jnp.where(core == 0, ZDIM - 1, 1), jnp.where(core == 0, ZDIM - 2, 2)),
    )


def gather_body(*refs):
    pieces, (kept_ref, given_ref, *single_refs) = refs[:YDIM], refs[YDIM:]
    me = lax.axis_index("beam")
    y, z = me // ZDIM, lax.rem(me, ZDIM)
    lane = lax.broadcasted_iota(jnp.int32, (TILE, 128), 1) // 32

    def block(far):
        target = lax.rem(z + far, ZDIM)
        merged = pieces[0][target]
        for shift in range(1, YDIM):
            moved = pltpu.roll(pieces[shift][target], 128 - 32 * shift, 1)
            merged = jnp.where(lane == lax.rem(y - shift + YDIM, YDIM), moved, merged)
        return merged

    kept, given = paired(lax.rem(lax.axis_index("chan"), 2))
    for i in range(2):
        kept_ref[i] = block(kept[i])
        given_ref[i] = block(given[i])
    for far, single_ref in zip(SINGLES, single_refs):
        single_ref[...] = block(far)


def gather(pieces):
    single = jax.ShapeDtypeStruct((TILE, 128), jnp.float32)
    double = jax.ShapeDtypeStruct((2, TILE, 128), jnp.float32)
    return pl.pallas_call(
        gather_body,
        out_shape=[double] * 2 + [single] * len(SINGLES),
        compiler_params=SMALL,
        name="gather",
    )(*pieces)


def pair_body(kept_ref, got_ref, near_ref, far_ref):
    for i, out_ref in enumerate((near_ref, far_ref)):
        out_ref[0] = kept_ref[i]
        out_ref[1] = got_ref[i]


def pair(kept, got):
    return pl.pallas_call(
        pair_body,
        out_shape=[jax.ShapeDtypeStruct(kept.shape, jnp.float32)] * 2,
        compiler_params=SMALL,
        name="pair",
    )(kept, got)


def east_west(x_ref, p):
    v = [x_ref[:, e * 32 + p * 16 : e * 32 + p * 16 + 16, :].astype(jnp.float32) for e in range(4)]
    re, im = [a[:, :TILE] for a in v], [a[:, TILE:] for a in v]
    even_re, odd_re, diff_re, turn_re = re[0] + re[2], re[1] + re[3], re[0] - re[2], re[1] - re[3]
    even_im, odd_im, diff_im, turn_im = im[0] + im[2], im[1] + im[3], im[0] - im[2], im[1] - im[3]
    real = (even_re + odd_re, diff_re + turn_im, even_re - odd_re, diff_re - turn_im)
    imag = (even_im + odd_im, diff_im - turn_re, even_im - odd_im, diff_im + turn_re)
    tidy = lambda beams: [beam.astype(jnp.bfloat16).reshape(FEEDS, 128) for beam in beams]
    return tidy(real), tidy(imag)


def squares(a, b):
    return a * a + b * b


def bin_squares(sums):
    sums = sums.reshape(NSBIN // 16, 2, 8, 256)
    cos_re, cos_im = sums[:, 0, :, :128], sums[:, 0, :, 128:]
    sin_re, sin_im = sums[:, 1, :, :128], sums[:, 1, :, 128:]
    plus = squares(cos_re + sin_im, cos_im - sin_re)
    minus = squares(cos_re - sin_im, cos_im + sin_re)
    top = lax.broadcasted_iota(jnp.int32, (8, 128), 0) == 0
    plus_top = jnp.where(top, squares(cos_re[0], cos_im[0]), plus[0])[None]
    minus_top = jnp.where(top, squares(sin_re[0], sin_im[0]), minus[0])[None]
    return jnp.concatenate([plus_top, plus[1:], minus_top, minus[1:]], axis=0)


def bin_power(table_ref, pols, k):
    (real0, imag0), (real1, imag1) = pols
    feeds = jnp.concatenate([real0[k], imag0[k], real1[k], imag1[k]], axis=1)
    sums = jnp.dot(table_ref[...], feeds, preferred_element_type=jnp.float32)
    return (bin_squares(sums[:, :256]) + bin_squares(sums[:, 256:])).reshape(NSBIN, 128)


def frame_sums(bins, channel):
    parts = [half for power in bins for half in split_bf16(power)]
    row = lax.broadcasted_iota(jnp.int32, (len(parts) * 128, 128), 0)
    lane = lax.broadcasted_iota(jnp.int32, (len(parts) * 128, 128), 1)
    target = channel * 32 + row % 128 // FLEN * 4 + row // 256
    summing = jnp.where(lane == target, 1.0 / (8.0 * FLEN), 0.0).astype(jnp.bfloat16)
    return jnp.dot(
        jnp.concatenate(parts, axis=1), summing, preferred_element_type=jnp.float32
    )


def power_body(x_ref, table_ref, out_ref):
    power = jnp.zeros((NSBIN, 128), jnp.float32)
    for channel in range(OWNED):
        one = x_ref.at[:, channel * ROWS : (channel + 1) * ROWS]
        pols = [east_west(one, p) for p in range(2)]
        power += frame_sums([bin_power(table_ref, pols, k) for k in range(4)], channel)
    out_ref[...] = power


def channel_power(voltages, table):
    return pl.pallas_call(
        power_body,
        in_specs=[pl.BlockSpec(memory_space=pltpu.VMEM)] * 2,
        out_specs=pl.BlockSpec(memory_space=pltpu.VMEM),
        out_shape=jax.ShapeDtypeStruct((NSBIN, 128), jnp.float32),
        compiler_params=pltpu.CompilerParams(vmem_limit_bytes=VMEM_LIMIT),
        cost_estimate=pl.CostEstimate(
            flops=3_000_000_000, bytes_accessed=6 * 2**20, transcendentals=0
        ),
        name="channel_power",
    )(voltages, table)


def regrid_body(power_ref, *refs):
    near_ref, far_ref, near_swap_ref, far_swap_ref, *single_refs, out_ref, param_ref = refs
    z = lax.rem(lax.axis_index("beam"), ZDIM)
    kept, given = paired(lax.rem(lax.axis_index("chan"), 2))
    blocks = [(kept[0], near_ref[0]), (kept[1], far_ref[0])]
    blocks += [(given[0], near_swap_ref[1]), (given[1], far_swap_ref[1])]
    blocks += [(far, single_ref[...]) for far, single_ref in zip(SINGLES, single_refs)]
    for far, block in blocks:
        param_ref[lax.rem(z - far + ZDIM, ZDIM)] = block
    halves = jnp.concatenate(split_bf16(power_ref[...]), axis=1)
    halves = jnp.concatenate([halves, halves], axis=0)
    params = param_ref[...].reshape(ZDIM * TILE, 128)
    column = lax.broadcasted_iota(jnp.int32, (ZDIM * TILE, NSBIN), 1)
    bins = jnp.where(column <= NSBIN // 2, column, 3 * NSBIN // 2 - column)
    place = lax.broadcasted_iota(jnp.int32, (NSBEAM, 128), 1) // 32
    out = jnp.zeros((NSBEAM, 128), jnp.float32)
    for channel in range(OWNED):
        tiles = []
        for y in range(YDIM):
            lane = 32 * y + channel
            offset = bins - params[:, lane : lane + 1].astype(jnp.int32)
            grid = jnp.zeros((ZDIM * TILE, NSBIN), jnp.float32)
            for m in range(MAXBIN):
                lane += OWNED
                grid = jnp.where(offset == m, params[:, lane : lane + 1], grid)
            tiles.append(jnp.concatenate(split_bf16(grid), axis=1))
        beams = jnp.dot(
            jnp.concatenate(tiles, axis=0), halves, preferred_element_type=jnp.float32
        )
        out = jnp.where(place == channel, beams[:, :128] + beams[:, 128:], out)
    out_ref[...] = out


def regrid(power, pieces):
    return pl.pallas_call(
        regrid_body,
        out_shape=jax.ShapeDtypeStruct((NSBEAM, 128), jnp.float32),
        scratch_shapes=[pltpu.VMEM((ZDIM, TILE, 128), jnp.float32)],
        compiler_params=pltpu.CompilerParams(vmem_limit_bytes=VMEM_LIMIT),
        name="regrid",
    )(power, *pieces)


def flatten_body(beams_ref, sums_ref, out_ref):
    total = jnp.sum(sums_ref[...], axis=0)
    total = total + pltpu.roll(total, 64, 1)
    total = total + pltpu.roll(total, 32, 1)
    flat = beams_ref[...] / (total / CHANNELS + 1e-06)[None]
    lane = lax.broadcasted_iota(jnp.int32, (32, 128), 1) % OWNED
    for j in range(TILE):
        turned = jnp.repeat(flat[:, j, :], OWNED, axis=0).T
        picked = jnp.zeros((32, 128), jnp.float32)
        for ch in range(OWNED):
            picked = jnp.where(lane == ch, turned[ch * 32 : ch * 32 + 32], picked)
        out_ref[:, j, :] = picked


def flatten(beams, sums):
    return pl.pallas_call(
        flatten_body,
        out_shape=jax.ShapeDtypeStruct((32, TILE, 128), jnp.float32),
        compiler_params=SMALL,
        name="flatten",
    )(beams, sums)


def along_z(block, far):
    pairs = [
        (y * ZDIM + z, y * ZDIM + (z + far) % ZDIM) for y in range(YDIM) for z in range(ZDIM)
    ]
    return lax.ppermute(block, "beam", pairs)


def both_ways(block, far):
    pairs = []
    for g in range(lax.axis_size("chan")):
        for y in range(YDIM):
            for z in range(ZDIM):
                to = (z + far if g % 2 == 0 else z - far) % ZDIM
                pairs.append(((g * YDIM + y) * ZDIM + z, (g * YDIM + y) * ZDIM + to))
    return lax.ppermute(block, ("chan", "beam"), pairs)


def swap(block):
    return lax.ppermute(block, "chan", [(g, g ^ 1) for g in range(lax.axis_size("chan"))])


def shards(voltages, bin_range, weights, bandpass):
    volts = lax.all_to_all(
        voltages.reshape(PEERS, OWNED * ROWS, 128), "beam", 0, 0, tiled=True
    )
    params = pack(bin_range, weights, bandpass)
    pieces = [params] + [
        lax.ppermute(params, "beam", [(i, (i + shift * ZDIM) % PEERS) for i in range(PEERS)])
        for shift in range(1, YDIM)
    ]
    kept, given, *singles = gather(pieces)
    near, far = pair(kept, swap(given))
    near, far = both_ways(near, 1), both_ways(far, 2)
    singles[1:] = [along_z(single, dist) for single, dist in zip(singles[1:], SINGLES[1:])]
    parts = [near, far, swap(near), swap(far)] + singles
    power = channel_power(volts, ns_table())
    beams = regrid(power, parts)
    beams = lax.all_to_all(beams.reshape(PEERS, TILE, 128), "beam", 0, 0, tiled=True)
    sums = jnp.broadcast_to(jnp.sum(beams, axis=0), (lax.axis_size("chan"), TILE, 128))
    sums = lax.all_to_all(sums, "chan", 0, 0, tiled=True)
    return flatten(beams, sums).reshape(8, 4, TILE, 128)


def solution(mesh):
    return jax.shard_map(
        shards,
        mesh=mesh,
        in_specs=(
            P("chan", None, None, None, "beam", None),
            P(None, "beam", "chan"),
            P(None, "beam", "chan"),
            P("chan"),
        ),
        out_specs=P(None, None, "beam", "chan"),
        check_vma=False,
    )
```
